32 devices in a mesh: section: 2 (over core), dp: 16 (over z, y, x).
Axes of the slice: x: 2, y: 2, z: 4, core: 2. Of those that a mesh axis runs over, the one named last changes fastest.
Arguments:
- enc_input: bfloat16 [256, 96, 512], P('dp'), may hold values from -6 to 6
- dec_input: bfloat16 [256, 144, 512], P('dp'), may hold values from -6 to 6
- pred_grad: float32 [256, 144, 321], P('dp'), may hold values from -6 to 6
- dataset_id: int32 [256], P('dp'), may hold values from 0 to 2
- chan_mask: int32 [256, 321], P('dp'), may hold values 0 or 1
- enc_modes: int32 [64], replicated, may hold values from 0 to 48, as said below
- dec_modes: int32 [64], replicated, may hold values from 0 to 72, as said below
- proj_query: bfloat16 [2, 512, 512], P('section'), may hold values from -0.25 to 0.25
- mix_self: bfloat16 [2, 8, 4096, 128], P('section'), may hold values from -0.5 to 0.5
- proj_output: bfloat16 [2, 512, 512], P('section'), may hold values from -0.25 to 0.25
- ffn_inner: bfloat16 [2, 512, 2048], P('section'), may hold values from -0.25 to 0.25
- ffn_outer: bfloat16 [2, 2048, 512], P('section'), may hold values from -0.125 to 0.125
- cross_query: bfloat16 [512, 512], P('section'), may hold values from -0.25 to 0.25
- cross_key: bfloat16 [512, 512], P('section'), may hold values from -0.25 to 0.25
- cross_output: bfloat16 [512, 512], P('section'), may hold values from -0.25 to 0.25
- mix_cross: bfloat16 [8, 4096, 128], P('section'), may hold values from -0.5 to 0.5
- trend_weight: bfloat16 [3, 512, 321], P(None, 'section'), may hold values from -0.15625 to 0.15625
- season_weight: bfloat16 [512, 321], P('section'), may hold values from -0.25 to 0.25
Outputs:
- predictions: float32 [256, 144, 321], P('dp', 'section')
- trends: float32 [256, 144, 321], P('dp', 'section')
- enc_input_grad: float32 [256, 96, 512], P('dp', 'section')
- dec_input_grad: float32 [256, 144, 512], P('dp', 'section')
- grad_proj_query: float32 [2, 512, 512], P('section', 'dp')
- grad_mix_self: float32 [2, 8, 4096, 128], P('section', None, 'dp')
- grad_proj_output: float32 [2, 512, 512], P('section', 'dp')
- grad_ffn_inner: float32 [2, 512, 2048], P('section', 'dp')
- grad_ffn_outer: float32 [2, 2048, 512], P('section', 'dp')
- grad_cross_query: float32 [512, 512], P(('section', 'dp'))
- grad_cross_key: float32 [512, 512], P(('section', 'dp'))
- grad_cross_output: float32 [512, 512], P(('section', 'dp'))
- grad_mix_cross: float32 [8, 4096, 128], P('section', 'dp')
- grad_trend_weight: float32 [3, 512, 321], P(None, ('section', 'dp'))
- grad_season_weight: float32 [512, 321], P(('section', 'dp'))
The draws below stay inside these ranges and needn't reach their ends.
Inputs may be any that keep to these rules, and one draw needn't show every extreme that they name: `enc_modes`: indices may repeat; 0 and 48 both occur. `dec_modes`: indices may repeat; 0 and 72 both occur. `dataset_id`: 0, 1, 2 for the sets of 7, 321 and 21 variates. `chan_mask`: 1 where a variate is observed.
All inputs are finite; a program needn't handle non-finite values. No bound on the sum of `chan_mask` on one device may be relied on, other than what follows from the above.
Results may differ from the reference program's by a relative error of at most 0.035.
Values may be sent and summed in bfloat16 or wider, within the bound.
No kernel may reach another device: no remote copies, remote signals or barrier semaphores. Data moves between devices by JAX's collectives and lax.ppermute only.
A program may use at most 960 MiB of HBM per device.

```python
import math
import jax
import jax.numpy as jnp
from jax import lax

D = 512
HEADS = 8
HEAD = 64
FF = 2048
MODES = 64
VARIATES = 321
ENC_LEN = 96
DEC_LEN = 144
SPAN = 25
IT_DEV = 16
ITEMS = 256
N_SECTION = 2
N_DP = 16


def mode_indices(key, top_value):
    first_key, second_key = jax.random.split(key)
    picked = jax.random.randint(first_key, (MODES,), 0, top_value + 1)
    picked = picked.at[0].set(0).at[1].set(top_value)
    return jax.random.permutation(second_key, picked)


def draw_enc_modes(key, part):
    key = jax.random.fold_in(key, 11)
    return mode_indices(key, ENC_LEN // 2)


def draw_dec_modes(key, part):
    key = jax.random.fold_in(key, 12)
    return mode_indices(key, DEC_LEN // 2)


def place_ends(drawn, key, low, high):
    index_at = [jax.random.randint(jax.random.fold_in(key, axis), (), 0, length) for axis, length in enumerate(drawn.shape)]
    longest = drawn.shape.index(max(drawn.shape))
    next_to = index_at[:longest] + [(index_at[longest] + 1) % drawn.shape[longest]] + index_at[longest + 1:]
    return drawn.at[tuple(index_at)].set(low).at[tuple(next_to)].set(high)


def level_of(key, extent, pieces, low, largest):
    factor_of, own = 1.0, jax.random.fold_in(key, 6)
    for axis_at, parts in pieces:
        draws = jnp.exp(jax.random.uniform(jax.random.fold_in(own, axis_at), (parts,), jnp.float32, low / len(pieces), largest / len(pieces)))
        factor_of = factor_of * jnp.repeat(draws, extent[axis_at] // parts).reshape([-1 if axis == axis_at else 1 for axis in range(len(extent))])
    return factor_of


def noise(rng, dims, spread, limit, cuts=(), kind=jnp.bfloat16):
    values = jax.random.normal(rng, dims, jnp.float32) * spread
    if len(cuts) > 0:
        values = level_of(rng, dims, cuts, -0.22, 0.18) * values
    return jnp.clip(values, min=-limit, max=limit).astype(kind)


def setup_inputs(seed: int = 0) -> dict:
    keys = jax.random.split(jax.random.key(seed), 19)
    return {
        "enc_input": noise(keys[0], (ITEMS, ENC_LEN, D), 1.0, 6.0, ((0, 16),)),
        "dec_input": noise(keys[1], (ITEMS, DEC_LEN, D), 1.0, 6.0, ((0, 16),)),
        "pred_grad": noise(keys[2], (ITEMS, DEC_LEN, VARIATES), 1.0, 6.0, ((0, 16),), jnp.float32),
        "dataset_id": place_ends(jax.random.randint(keys[3], (ITEMS,), 0, 3), jax.random.fold_in(keys[3], 1), 0, 2).astype(jnp.int32),
        "chan_mask": place_ends((jax.random.randint(keys[4], (ITEMS, VARIATES), 0, 4) < 3).astype(jnp.int32), jax.random.fold_in(keys[4], 1), 0, 1),
        "enc_modes": draw_enc_modes(jax.random.fold_in(keys[18], 71), 0),
        "dec_modes": draw_dec_modes(jax.random.fold_in(keys[18], 71), 0),
        "proj_query": noise(keys[7], (N_SECTION, D, D), D ** -0.5, 0.25, ((0, 2),)),
        "mix_self": noise(keys[8], (N_SECTION, HEADS, MODES * HEAD, 2 * HEAD), (2 * HEAD) ** -0.5, 0.5, ((0, 2),)),
        "proj_output": noise(keys[9], (N_SECTION, D, D), D ** -0.5, 0.25, ((0, 2),)),
        "ffn_inner": noise(keys[10], (N_SECTION, D, FF), D ** -0.5, 0.25, ((0, 2),)),
        "ffn_outer": noise(keys[11], (N_SECTION, FF, D), FF ** -0.5, 0.125, ((0, 2),)),
        "cross_query": noise(keys[12], (D, D), D ** -0.5, 0.25, ((0, 2),)),
        "cross_key": noise(keys[13], (D, D), D ** -0.5, 0.25, ((0, 2),)),
        "cross_output": noise(keys[14], (D, D), D ** -0.5, 0.25, ((0, 2),)),
        "mix_cross": noise(keys[15], (HEADS, MODES * HEAD, 2 * HEAD), (2 * HEAD) ** -0.5, 0.5, ((0, 2),)),
        "trend_weight": noise(keys[16], (3, D, VARIATES), (3 * D) ** -0.5, 0.15625, ((1, 2),)),
        "season_weight": noise(keys[17], (D, VARIATES), D ** -0.5, 0.25, ((0, 2),)),
    }


@jax.custom_vjp
def low(v):
    return lax.optimization_barrier(v.astype(jnp.bfloat16)).astype(jnp.float32)

@jax.custom_vjp
def low_back(v):
    return v

def low_keep(v):
    return (low(v), None)

def low_pass(kept, grad):
    return (grad,)

def back_keep(v):
    return (v, None)

def back_low(kept, grad):
    return (low(grad),)
low.defvjp(low_keep, low_pass)
low_back.defvjp(back_keep, back_low)
highest = lax.Precision.HIGHEST

def round_both(values):
    return low(low_back(values))

def dense_product(values, weight):
    return jnp.einsum('bld,de->ble', values, weight, precision=highest)

def transform_tables(indices, length):
    positions = jnp.arange(length, dtype=jnp.int32)
    phase_index = positions[:, None] * indices[None, :].astype(jnp.int32) % length
    angles = 2.0 * math.pi / length * phase_index.astype(jnp.float32)
    cosine = jnp.cos(angles)
    sine_part = jnp.sin(angles)
    forward_table = jnp.stack([cosine, -sine_part], axis=-1) / math.sqrt(length)
    inverse_table = jnp.stack([cosine.T, -sine_part.T], axis=1) * math.sqrt(2.0 / length)
    return (low(forward_table), low(inverse_table))

def average_matrix(length):
    positions = jnp.arange(length, dtype=jnp.int32)
    offsets = jnp.arange(SPAN, dtype=jnp.int32) - SPAN // 2
    sources = jnp.clip(positions[:, None] + offsets[None, :], 0, length - 1)
    counted = lax.optimization_barrier(jnp.sum((sources[:, :, None] == positions[None, None, :]).astype(jnp.float32), axis=1))
    return counted / SPAN

def decompose(stream, matrix):
    trend = jnp.einsum('ts,bsd->btd', matrix, stream, precision=highest)
    return (stream - trend, trend)

def spectrum(values, forward_table):
    batch_size, length, model_width = values.shape
    split_heads = values.reshape(batch_size, length, HEADS, model_width // HEADS)
    result = jnp.einsum('bthe,tmc->bhmce', split_heads, forward_table, precision=highest)
    return result.reshape(batch_size, HEADS, forward_table.shape[1], -1)

def synthesis(coeffs, inverse_table):
    batch_size = coeffs.shape[0]
    split_parts = coeffs.reshape(batch_size, HEADS, coeffs.shape[2], 2, -1)
    result = jnp.einsum('bhmco,mct->btho', split_parts, inverse_table, precision=highest)
    return result.reshape(batch_size, inverse_table.shape[2], -1)

def mixing_matrix(weight):
    half_width = weight.shape[2] // 2
    shaped = weight.reshape(weight.shape[0], -1, half_width, 2 * half_width)
    lower_rows = jnp.concatenate([-shaped[..., half_width:], shaped[..., :half_width]], axis=-1)
    return jnp.concatenate([shaped, lower_rows], axis=2)

def mixing_apply(coeffs, matrix):
    return jnp.einsum('bhmf,hmfg->bhmg', coeffs, matrix, precision=highest)

def rotate(coeffs):
    half_width = coeffs.shape[-1] // 2
    return jnp.concatenate([-coeffs[..., half_width:], coeffs[..., :half_width]], axis=-1)

def self_block(stream, query_weight, mix_weight, output_weight, tables):
    queries = round_both(dense_product(low(stream), query_weight))
    coeffs = round_both(spectrum(queries, tables[0]))
    mixed = round_both(mixing_apply(coeffs, mixing_matrix(mix_weight)))
    series = round_both(synthesis(mixed, tables[1]))
    return low_back(dense_product(series, output_weight))

def cross_block(stream, memory, query_weight, key_weight, mix_weight, output_weight, dec_tables, enc_tables):
    queries = round_both(dense_product(low(stream), query_weight))
    keys_part = round_both(dense_product(memory, key_weight))
    query_coeffs = round_both(spectrum(queries, dec_tables[0]))
    key_coeffs = round_both(spectrum(keys_part, enc_tables[0]))
    half_width = key_coeffs.shape[-1] // 2
    key_real = key_coeffs[..., :half_width]
    key_imag = key_coeffs[..., half_width:]
    key_conj = jnp.concatenate([key_real, -key_imag], axis=-1)
    key_swap = jnp.concatenate([key_imag, key_real], axis=-1)
    score_scale = 1.0 / math.sqrt(HEAD)
    value_scale = 1.0 / math.sqrt(MODES)
    real_score = low_back(jnp.einsum('bhxf,bhyf->bhxy', query_coeffs, key_conj, precision=highest) * score_scale)
    imag_score = low_back(jnp.einsum('bhxf,bhyf->bhxy', query_coeffs, key_swap, precision=highest) * score_scale)
    attend = low(jnp.concatenate([jnp.tanh(real_score), jnp.tanh(imag_score)], axis=-1))
    key_block = jnp.concatenate([key_coeffs, rotate(key_coeffs)], axis=2)
    values_part = round_both(jnp.einsum('bhxy,bhyf->bhxf', attend, key_block, precision=highest) * value_scale)
    mixed = round_both(mixing_apply(values_part, mixing_matrix(mix_weight)))
    series = round_both(synthesis(mixed, dec_tables[1]))
    return low_back(dense_product(series, output_weight))

def feed_forward(stream, inner_weight, outer_weight):
    before = low_back(dense_product(low(stream), inner_weight))
    hidden = low(jax.nn.gelu(before))
    return low_back(dense_product(hidden, outer_weight))

def encoder(stream, core, tables, matrix):
    query_weight, mix_weight, output_weight, inner_weight, outer_weight = core
    season_one = decompose(stream + self_block(stream, query_weight, mix_weight, output_weight, tables), matrix)[0]
    season_two = decompose(season_one + feed_forward(season_one, inner_weight, outer_weight), matrix)[0]
    return round_both(season_two)

def decoder(stream, memory, core, extras, dec_tables, enc_tables, matrix, valid_cols):
    query_weight, mix_weight, output_weight, inner_weight, outer_weight = core
    cross_query, cross_key, cross_output, cross_mix, trend_weight, season_weight = extras
    season_one, trend_one = decompose(stream + self_block(stream, query_weight, mix_weight, output_weight, dec_tables), matrix)
    cross_out = cross_block(season_one, memory, cross_query, cross_key, cross_mix, cross_output, dec_tables, enc_tables)
    season_two, trend_two = decompose(season_one + cross_out, matrix)
    season_three, trend_three = decompose(season_two + feed_forward(season_two, inner_weight, outer_weight), matrix)
    trend_sum = low(trend_one + trend_two + trend_three)
    trend_taps = jnp.concatenate([jnp.roll(trend_sum, 1, axis=1), trend_sum, jnp.roll(trend_sum, -1, axis=1)], axis=-1)
    trend_part = low_back(dense_product(trend_taps, trend_weight.reshape(-1, trend_weight.shape[-1])))
    season_part = low_back(dense_product(low(season_three), season_weight))
    keep_mask = valid_cols[:, None, :]
    return ((season_part + trend_part) * keep_mask, trend_part * keep_mask)

def valid_mask(dataset_id, chan_mask, columns_total):
    widths = 7 * (dataset_id == 0) + 321 * (dataset_id == 1) + 21 * (dataset_id == 2)
    columns = jnp.arange(columns_total, dtype=jnp.int32)
    return ((columns[None, :] < widths[:, None]) & (chan_mask == 1)).astype(jnp.float32)

def reference(enc_input, dec_input, pred_grad, dataset_id, chan_mask, enc_modes, dec_modes, proj_query, mix_self, proj_output, ffn_inner, ffn_outer, cross_query, cross_key, cross_output, mix_cross, trend_weight, season_weight):
    stacked = tuple((weight.astype(jnp.float32) for weight in (proj_query, mix_self, proj_output, ffn_inner, ffn_outer)))
    extras = tuple((weight.astype(jnp.float32) for weight in (cross_query, cross_key, cross_output, mix_cross, trend_weight, season_weight)))
    enc_tables = transform_tables(enc_modes, ENC_LEN)
    dec_tables = transform_tables(dec_modes, DEC_LEN)
    enc_average = average_matrix(ENC_LEN)
    dec_average = average_matrix(DEC_LEN)
    valid_cols = valid_mask(dataset_id, chan_mask, VARIATES)

    def regroup(array):
        return array.reshape((N_DP, IT_DEV) + array.shape[1:])

    def group_step(totals, group):
        enc_rows, dec_rows, cotangent, valid_rows = group

        def forward(enc_values, dec_values, stacked_weights, extra_weights):
            memory = encoder(enc_values, tuple((weight[0] for weight in stacked_weights)), enc_tables, enc_average)
            return decoder(dec_values, memory, tuple((weight[1] for weight in stacked_weights)), extra_weights, dec_tables, enc_tables, dec_average, valid_rows)
        outputs, pullback = jax.vjp(forward, enc_rows.astype(jnp.float32), dec_rows.astype(jnp.float32), stacked, extras)
        enc_grad, dec_grad, stacked_grad, extra_grad = pullback((cotangent, jnp.zeros_like(outputs[1])))
        totals = jax.tree.map(jnp.add, totals, (stacked_grad, extra_grad))
        return (totals, (outputs[0], outputs[1], enc_grad, dec_grad))
    start = jax.tree.map(jnp.zeros_like, (stacked, extras))
    totals, results = lax.scan(group_step, start, (regroup(enc_input), regroup(dec_input), regroup(pred_grad), regroup(valid_cols)))
    flats = tuple((result.reshape((-1,) + result.shape[2:]) for result in results))
    core_grads, extra_grads = totals
    return (flats[0], flats[1], flats[2], flats[3], core_grads[0], core_grads[1], core_grads[2], core_grads[3], core_grads[4], extra_grads[0], extra_grads[1], extra_grads[2], extra_grads[3], extra_grads[4], extra_grads[5])
```

```python
import math

import jax
import jax.numpy as jnp
import numpy as np
from jax import lax
from jax.experimental import pallas as pl
from jax.experimental.pallas import tpu as pltpu
from jax.sharding import PartitionSpec as P

HEADS = 8
SPAN = 25
PIECES = 16
ROWS = 768
CUT = 384
WIDE = 384
VMEM = 60 * 1024 * 1024

bf = jnp.bfloat16
f32 = jnp.float32


def mm(a, b):
    return lax.dot_general(a, b, (((1,), (0,)), ((), ())), preferred_element_type=f32)


def mm_nt(a, b):
    return lax.dot_general(a, b, (((1,), (1,)), ((), ())), preferred_element_type=f32)


def mm_tn(a, b):
    return lax.dot_general(a, b, (((0,), (0,)), ((), ())), preferred_element_type=f32)


def lower_lanes(shape):
    return lax.broadcasted_iota(jnp.int32, shape, len(shape) - 1) < 64


def turn(value):
    return pltpu.roll(value, 64, len(value.shape) - 1)


def transform_tables(indices, length):
    positions = jnp.arange(length, dtype=jnp.int32)
    phase = positions[:, None] * indices[None, :] % length
    angles = 2.0 * math.pi / length * phase.astype(f32)
    waves = jnp.concatenate([jnp.cos(angles), -jnp.sin(angles)], axis=1)
    forward = (waves / math.sqrt(length)).astype(bf)
    inverse = (waves * math.sqrt(2.0 / length)).astype(bf)
    return forward, forward.T, inverse, inverse.T


def average_counts(length):
    positions = np.arange(length)
    offsets = np.arange(SPAN) - SPAN // 2
    sources = np.clip(positions[:, None] + offsets[None, :], 0, length - 1)
    counts = np.sum(sources[:, :, None] == positions[None, None, :], axis=1)
    return jnp.asarray(counts, bf), jnp.asarray(counts.T, bf)


def items_to_modes(load, store, modes):
    def step(j, carry):
        store(j, jnp.concatenate([load(j), load(modes + j)], axis=0).astype(bf))
        return carry

    lax.fori_loop(0, modes, step, 0, unroll=8)


def modes_to_items(source, scratch, base, items, modes):
    def step(j, carry):
        value = source[j].astype(f32)
        for k in range(scratch.shape[0]):
            lanes = slice(k * 128, (k + 1) * 128)
            scratch[k, pl.ds(base + j, items, stride=2 * modes), :] = value[:items, lanes]
            scratch[k, pl.ds(base + modes + j, items, stride=2 * modes), :] = value[items:, lanes]
        return carry

    lax.fori_loop(0, modes, step, 0, unroll=8)


def set_rows(scratch, rows, value):
    for k in range(scratch.shape[0]):
        scratch[k, rows, :] = value[:, k * 128 : (k + 1) * 128]


def get_rows(scratch, rows):
    return jnp.concatenate([scratch[k, rows, :] for k in range(scratch.shape[0])], axis=1)


def season_of(stream, counts, length, items):
    low = stream.astype(bf)
    parts = [mm(counts, low[i * length : (i + 1) * length]) for i in range(items)]
    return jnp.concatenate(parts, axis=0) * (1.0 / SPAN)


def gelu_pair(pre):
    c = math.sqrt(2.0 / math.pi)
    square = pre * pre
    t = jnp.tanh(c * pre * (1.0 + 0.044715 * square))
    half = 0.5 * (1.0 + t)
    slope = half + 0.5 * pre * (1.0 - t * t) * (c * (1.0 + 3.0 * 0.044715 * square))
    return (pre * half).astype(bf), slope.astype(bf)


def ffn_forward(low, w1, w2, hidden, slope, rows):
    width = w1.shape[1] // 4
    for n in range(4):
        cols = slice(n * width, (n + 1) * width)
        h, g = gelu_pair(mm(low, w1[:, cols]))
        hidden[rows, cols] = h
        slope[rows, cols] = g
    return mm(hidden[rows, :], w2[...])


def ffn_backward(low_grad, w1, w2, slope, pre_grad, rows):
    width = w1.shape[1] // 4
    for n in range(4):
        cols = slice(n * width, (n + 1) * width)
        value = mm_nt(low_grad, w2[cols, :]) * slope[rows, cols].astype(f32)
        pre_grad[rows, cols] = value.astype(bf)
    return mm_nt(pre_grad[rows, :], w1[...])


class Sender:
    def __init__(self, sc, buffer, cut):
        self.sc, self.buffer, self.cut = sc, buffer, cut
        self.place = [sc[0], 1 - sc[0]]

    def put(self, owner, dest, row, value):
        at = self.sc[1 + dest] if row < self.cut else self.sc[1 + PIECES + dest]
        rows = pl.ds(row, value.shape[0])
        self.buffer[self.place[owner], at, rows, :] = value.astype(bf)

    def halves(self, row, value):
        part = value.shape[0] // (2 * PIECES)
        for owner in range(2):
            for dest in range(PIECES):
                start = (owner * PIECES + dest) * part
                for lane in range(value.shape[1] // 128):
                    block = value[start : start + part, lane * 128 : (lane + 1) * 128]
                    self.put(owner, dest, row + lane * part, block)

    def whole(self, owner, row, value):
        part = value.shape[0] // PIECES
        for dest in range(PIECES):
            for lane in range(value.shape[1] // 128):
                block = value[dest * part : (dest + 1) * part, lane * 128 : (lane + 1) * 128]
                self.put(owner, dest, row + lane * part, block)

    def ffn(self, row, low_t, grad_t, pre_grad, hidden):
        part = low_t.shape[0] // PIECES
        for n in range(PIECES // 2):
            cols = slice(n * 256, (n + 1) * 256)
            inner = mm(low_t[...], pre_grad[:, cols])
            outer = mm(grad_t[...], hidden[:, cols])
            for k in range(2):
                lane = 2 * n + k
                lanes = slice(k * 128, (k + 1) * 128)
                for dest in range(PIECES):
                    block = inner[dest * part : (dest + 1) * part, lanes]
                    self.put(0, dest, row + lane * part, block)
                first = self.cut - row
                self.put(1, lane, row, outer[:first, lanes])
                self.put(1, lane, self.cut, outer[first:, lanes])

    def send(self, keep, give, sems):
        copies = [
            pltpu.make_async_copy(self.buffer.at[i], target, sems.at[i])
            for i, target in enumerate((keep, give))
        ]
        for copy in copies:
            copy.start()
        for copy in copies:
            copy.wait()


def spectrum_kernel(sc, xe, xd, we, wd, fte, ftd, own, give, scratch):
    items = own.shape[1] // 2
    modes = own.shape[0]
    span = items * 2 * modes
    for layer, (x, w, ft) in enumerate(((xe, we, fte), (xd, wd, ftd))):
        length = ft.shape[1]
        for g in range(2):
            count = items // 2
            q = mm(x[g * count * length : (g + 1) * count * length], w[...]).astype(bf)
            for i in range(count):
                at = layer * span + (g * count + i) * 2 * modes
                value = mm(ft[...], q[i * length : (i + 1) * length])
                set_rows(scratch, slice(at, at + 2 * modes), value)
    to_partner(sc[0], scratch, own, give, span, items, modes)


def mix_kernel(w, x_own, x_far, y_own, y_far):
    heads, count = w.shape[0], x_own.shape[0]
    items = x_own.shape[1] // 2
    low_b = lower_lanes((4 * items, 128))
    for j in range(count):
        for p in range(heads // 2):
            lanes = slice(p * 128, (p + 1) * 128)
            weight = jnp.concatenate(
                [w[2 * p, j * 64 : (j + 1) * 64, :], w[2 * p + 1, j * 64 : (j + 1) * 64, :]], axis=0
            )
            x = jnp.concatenate([x_own[j, :, lanes], x_far[j, :, lanes]], axis=0)
            zero = jnp.zeros_like(x)
            left = jnp.concatenate([jnp.where(low_b, x, zero), jnp.where(low_b, zero, x)], axis=0)
            product = mm(left, weight)
            a, b = product[: 4 * items], product[4 * items :]
            front = jnp.where(low_b, a, turn(b))
            back = jnp.where(low_b, turn(a), b)
            for k, target in ((0, y_own), (1, y_far)):
                real = slice(2 * k * items, (2 * k + 1) * items)
                imag = slice((2 * k + 1) * items, (2 * k + 2) * items)
                value = jnp.concatenate([front[real] - back[imag], back[real] + front[imag]], axis=0)
                target[j, :, lanes] = value.astype(bf)


def mix_back_kernel(places, w, x_own, x_far, g_own, g_far, dx_own, dx_far, dw_a, dw_b):
    heads, count = w.shape[0], x_own.shape[0]
    items = x_own.shape[1] // 2
    low = lower_lanes((2 * items, 128))
    for j in range(count):
        for p in range(heads // 2):
            lanes = slice(p * 128, (p + 1) * 128)
            rows = slice(j * 64, (j + 1) * 64)
            weight = jnp.concatenate([w[2 * p, rows, :], w[2 * p + 1, rows, :]], axis=0)

            def parts(one, two):
                a, b = one[j, :, lanes].astype(f32), two[j, :, lanes].astype(f32)
                real = jnp.concatenate([a[:items], b[:items]], axis=0)
                imag = jnp.concatenate([a[items:], b[items:]], axis=0)
                return real, imag

            xr, xi = parts(x_own, x_far)
            gr, gi = parts(g_own, g_far)
            tr, ti = turn(gr), turn(gi)
            grads = jnp.concatenate(
                [
                    jnp.where(low, gr, ti),
                    jnp.where(low, gi, -tr),
                    jnp.where(low, tr, gi),
                    jnp.where(low, ti, -gr),
                ],
                axis=0,
            ).astype(bf)
            back = mm_nt(grads, weight)
            n = 2 * items
            dr = jnp.where(low, back[:n], back[2 * n : 3 * n])
            di = jnp.where(low, back[n : 2 * n], back[3 * n :])
            for k, target in ((0, dx_own), (1, dx_far)):
                part = slice(k * items, (k + 1) * items)
                target[j, :, lanes] = jnp.concatenate([dr[part], di[part]], axis=0).astype(bf)
            zero = jnp.zeros_like(xr)
            coeffs = jnp.concatenate(
                [
                    jnp.where(low, xr, zero),
                    jnp.where(low, xi, zero),
                    jnp.where(low, zero, xr),
                    jnp.where(low, zero, xi),
                ],
                axis=0,
            ).astype(bf)
            dw = mm_tn(coeffs, grads).astype(bf)
            target, head = (dw_a, 2 * p) if 2 * p < heads // 2 else (dw_b, 2 * p - heads // 2)
            target[0, head, rows, :] = dw[:64]
            target[0, head + 1, rows, :] = dw[64:]


def attention_forward(q, k):
    modes = q.shape[0] // 2
    low = lower_lanes(k.shape)
    zero = jnp.zeros_like(k)
    both = jnp.concatenate([jnp.where(low, k, zero), jnp.where(low, zero, k)], axis=0)
    products = mm_nt(q, both)
    sign = jnp.where(lower_lanes((modes, 128)), -1.0, 1.0)
    scores, slopes, factors = [], [], []
    for h in range(2):
        block = products[:, h * 128 : (h + 1) * 128]
        act = jnp.tanh((block[:modes] + sign * turn(block[modes:])) * 0.125)
        scores.append(act.astype(bf))
        slopes.append((1.0 - act * act).astype(bf))
        factors.append(-sign * act)
        factors.append(turn(act))
    values = mm(jnp.concatenate(factors, axis=0).astype(bf), k)
    values = jnp.where(low, values[: 2 * modes], values[2 * modes :]) * 0.125
    return scores, slopes, values


def attention_backward(q, k, scores, slopes, dv):
    modes = q.shape[0] // 2
    low = lower_lanes(k.shape)
    zero = jnp.zeros_like(k)
    both = jnp.concatenate([jnp.where(low, k, zero), jnp.where(low, zero, k)], axis=0)
    products = mm_nt(dv, both)
    sign = jnp.where(lower_lanes((modes, 128)), 1.0, -1.0)
    lefts, factors = [], []
    for h in range(2):
        block = products[:, h * 128 : (h + 1) * 128]
        act_grad = (sign * block[:modes] + turn(block[modes:])) * 0.125
        grad = act_grad * slopes[h].astype(f32)
        t = jnp.concatenate([grad, sign * turn(grad)], axis=0).astype(bf)
        act = scores[h].astype(f32)
        u = jnp.concatenate([sign * act, turn(act)], axis=0).astype(bf)
        factors.append(t)
        lefts.append(jnp.concatenate([u, t], axis=0))
    dq = mm(jnp.concatenate(factors, axis=0), k)
    dq = jnp.where(low, dq[: 2 * modes], dq[2 * modes :]) * 0.125
    right = jnp.concatenate([dv, q], axis=0)
    dk = jnp.where(low, mm_tn(lefts[0], right), mm_tn(lefts[1], right)) * 0.125
    return dq, dk


def middle_kernel(
    sc, y_own, y_back, xe, xd, woe, wod, w1, w2, wck, wcq, ge, gd, fte, ftd, ae, ad,
    ye, yd, s1e, hidden, slope, memory, kc, s1d, t1d, qc, act, act_slope, v_own, v_give,
    scratch, halves,
):
    items, modes = y_own.shape[1] // 2, y_own.shape[0]
    span = items * 2 * modes
    s = sc[0]
    modes_to_items(y_own, scratch, s * span, items, modes)
    modes_to_items(y_back, scratch, (1 - s) * span, items, modes)
    count = items // 2
    for layer, (g, y) in enumerate(((ge, ye), (gd, yd))):
        length = g.shape[0]
        for i in range(items):
            at = layer * span + i * 2 * modes
            series = mm(g[...], get_rows(scratch, slice(at, at + 2 * modes)).astype(bf))
            y[i * length : (i + 1) * length, :] = series.astype(bf)

    length = ge.shape[0]
    n = count * length
    for g in range(2):
        rows = slice(g * n, (g + 1) * n)
        stream = xe[rows].astype(f32) + mm(ye[rows, :], woe[...])
        season = stream - season_of(stream, ae[...], length, count)
        low = season.astype(bf)
        s1e[rows, :] = low
        stream = season + ffn_forward(low, w1, w2, hidden, slope, rows)
        season = stream - season_of(stream, ae[...], length, count)
        mem = season.astype(bf)
        memory[rows, :] = mem
        keys = mm(mem, wck[...]).astype(bf)
        for i in range(count):
            kc[g * count + i] = mm(fte[...], keys[i * length : (i + 1) * length]).astype(bf)

    length = gd.shape[0]
    n = count * length
    for g in range(2):
        rows = slice(g * n, (g + 1) * n)
        stream = xd[rows].astype(f32) + mm(yd[rows, :], wod[...])
        trend = season_of(stream, ad[...], length, count)
        season = stream - trend
        s1d[rows, :] = season
        t1d[rows, :] = trend
        queries = mm(season.astype(bf), wcq[...]).astype(bf)
        for i in range(count):
            qc[g * count + i] = mm(ftd[...], queries[i * length : (i + 1) * length]).astype(bf)

    def attend(i, carry):
        for p in range(HEADS // 2):
            lanes = slice(p * 128, (p + 1) * 128)
            scores, slopes, values = attention_forward(qc[i, :, lanes], kc[i, :, lanes])
            for h in range(2):
                act[i, 2 * p + h] = scores[h]
                act_slope[i, 2 * p + h] = slopes[h]
            at = (p // 2) * span + i * 2 * modes
            halves[p % 2, pl.ds(pl.multiple_of(at, 2 * modes), 2 * modes), :] = values
        return carry

    lax.fori_loop(0, items, attend, 0)
    to_partner(s, halves, v_own, v_give, span, items, modes)


def to_partner(s, scratch, own, give, span, items, modes):
    for target, base in ((own, s * span), (give, (1 - s) * span)):

        def load(j, base=base):
            return get_rows(scratch, pl.ds(base + j, items, stride=2 * modes))

        def store(j, value, target=target):
            target[j] = value

        items_to_modes(load, store, modes)


def outputs_kernel(
    sc, y_own, y_back, s1, t1, wco, w1, w2, tw, sw, mask, cotangent, g, gt, a, at,
    pred_keep, pred_give, trend_keep, trend_give, dz2, du, gy_own, gy_give, keep, give,
    halves, yc, zs, ts, low2, hidden, slope, taps, us, low3, ds, grads, low_t, grad_t,
    line_a, line_b, buffer, sems,
):
    items, modes = y_own.shape[1] // 2, y_own.shape[0]
    span = items * 2 * modes
    length = g.shape[0]
    count = items // 2
    n = count * length
    s = sc[0]
    modes_to_items(y_own, halves, s * span, items, modes)
    modes_to_items(y_back, halves, (1 - s) * span, items, modes)
    for i in range(items):
        rows = slice(i * 2 * modes, (i + 1) * 2 * modes)
        far = slice(span + i * 2 * modes, span + (i + 1) * 2 * modes)
        coeffs = jnp.concatenate([get_rows(halves, rows), get_rows(halves, far)], axis=1).astype(bf)
        yc[i * length : (i + 1) * length, :] = mm(g[...], coeffs).astype(bf)

    variates = cotangent.shape[2]
    line_a[...] = jnp.zeros_like(line_a)
    for i in range(items):
        line_a[:, 0:variates] = cotangent[i] * mask[i : i + 1, :]
        value = line_a[...]
        rows = slice(i * length, (i + 1) * length)
        taps[rows, 0:WIDE] = pltpu.roll(value, length - 1, 0).astype(bf)
        taps[rows, WIDE : 2 * WIDE] = value.astype(bf)
        taps[rows, 2 * WIDE : 3 * WIDE] = pltpu.roll(value, 1, 0).astype(bf)

    def forward(k, carry):
        rows = pl.ds(pl.multiple_of(k * n, 16), n)
        stream = s1[rows, :] + mm(yc[rows, :], wco[...])
        trend = season_of(stream, a[...], length, count)
        season = stream - trend
        trend = t1[rows, :] + trend
        low = season.astype(bf)
        low2[rows, :] = low
        stream = season + ffn_forward(low, w1, w2, hidden, slope, rows)
        last = season_of(stream, a[...], length, count)
        u = (trend + last).astype(bf)
        low = (stream - last).astype(bf)
        us[rows, :] = u
        low3[rows, :] = low
        tapped = mm(u, tw[...])
        seasonal = mm(low, sw[...])
        half = length // 2
        for i in range(count):
            part = slice(i * length, (i + 1) * length)
            item = k * count + i
            total = (
                pltpu.roll(tapped[part, 0:WIDE], 1, 0)
                + tapped[part, WIDE : 2 * WIDE]
                + pltpu.roll(tapped[part, 2 * WIDE :], length - 1, 0)
            )
            valid = mask[pl.ds(item, 1), :]
            line_a[...] = total + seasonal[part]
            line_b[...] = total
            near = pl.ds(pl.multiple_of(s * half, 8), half)
            far = pl.ds(pl.multiple_of((1 - s) * half, 8), half)
            pred_keep[item] = line_a[near, 0:variates] * valid
            pred_give[item] = (line_a[far, 0:variates] * valid).astype(bf)
            trend_keep[item] = line_b[near, 0:variates] * valid
            trend_give[item] = (line_b[far, 0:variates] * valid).astype(bf)
        trend_grad = mm_nt(taps[rows, :], tw[...])
        du[rows, :] = trend_grad
        season_grad = mm_nt(taps[rows, WIDE : 2 * WIDE], sw[...])
        stream_grad = season_grad + season_of(trend_grad - season_grad, at[...], length, count)
        low = stream_grad.astype(bf)
        grads[rows, :] = low
        season_grad = stream_grad + ffn_backward(low, w1, w2, slope, slope, rows)
        stream_grad = season_grad + season_of(trend_grad - season_grad, at[...], length, count)
        dz2[rows, :] = stream_grad
        low = stream_grad.astype(bf)
        ds[rows, :] = low
        zs[rows, :] = mm_nt(low, wco[...]).astype(bf)
        return carry

    lax.fori_loop(0, 2, forward, 0)
    for i in range(items):
        spectra = mm(gt[...], zs[i * length : (i + 1) * length, :])
        for k in range(2):
            start = k * span + i * 2 * modes
            set_rows(halves, slice(start, start + 2 * modes), spectra[:, k * 256 : (k + 1) * 256])
    to_partner(s, halves, gy_own, gy_give, span, items, modes)

    low_t[...] = low2[...].T
    grad_t[...] = grads[...].T
    sender = Sender(sc, buffer, CUT)
    sender.ffn(256, low_t, grad_t, slope, hidden)
    sender.halves(0, mm_tn(yc[...], ds[...]))
    sender.halves(64, mm_tn(us[...], taps[...]))
    sender.halves(208, mm_tn(low3[...], taps[:, WIDE : 2 * WIDE]))
    sender.send(keep, give, sems)


def cross_back_kernel(
    sc, dv_own, dv_back, qc, kc, act, act_slope, s1d, dz2, du, memory, wcq, wck, fd, fe, adt, aet,
    yd, ye, wod, woe, gtd, gte, hidden, slope, s1e, w1, w2,
    dz1d, dz1e, gy_own, gy_give, keep, give,
    halves, scratch, dq_items, dk_items, dqs, dks, glow, pre_grad, low_t, grad_t, mem_grad, glow_e,
    buffer, sems,
):
    items, modes = dv_own.shape[1] // 2, dv_own.shape[0]
    span = items * 2 * modes
    dec, enc = fd.shape[0], fe.shape[0]
    count = items // 2
    s = sc[0]
    modes_to_items(dv_own, halves, s * span, items, modes)
    modes_to_items(dv_back, halves, (1 - s) * span, items, modes)

    def attend(i, carry):
        for p in range(HEADS // 2):
            lanes = slice(p * 128, (p + 1) * 128)
            at = (p // 2) * span + i * 2 * modes
            dv = halves[p % 2, pl.ds(pl.multiple_of(at, 2 * modes), 2 * modes), :].astype(bf)
            dq, dk = attention_backward(
                qc[i, :, lanes],
                kc[i, :, lanes],
                [act[i, 2 * p], act[i, 2 * p + 1]],
                [act_slope[i, 2 * p], act_slope[i, 2 * p + 1]],
                dv,
            )
            dq_items[i, :, lanes] = dq.astype(bf)
            dk_items[i, :, lanes] = dk.astype(bf)
        return carry

    lax.fori_loop(0, items, attend, 0)
    for i in range(items):
        dqs[i * dec : (i + 1) * dec, :] = mm(fd[...], dq_items[i]).astype(bf)
        dks[i * enc : (i + 1) * enc, :] = mm(fe[...], dk_items[i]).astype(bf)

    sender = Sender(sc, buffer, CUT)
    sender.halves(0, mm_tn(s1d[...].astype(bf), dqs[...]))
    sender.halves(64, mm_tn(memory[...], dks[...]))
    for k in range(2):
        rows = slice(k * count * dec, (k + 1) * count * dec)
        season_grad = dz2[rows, :] + mm_nt(dqs[rows, :], wcq[...])
        stream_grad = season_grad + season_of(du[rows, :] - season_grad, adt[...], dec, count)
        dz1d[rows, :] = stream_grad
        low = stream_grad.astype(bf)
        glow[rows, :] = low
        series = mm_nt(low, wod[...]).astype(bf)
        for i in range(count):
            start = span + (k * count + i) * 2 * modes
            value = mm(gtd[...], series[i * dec : (i + 1) * dec])
            set_rows(scratch, slice(start, start + 2 * modes), value)
    sender.whole(1, 128, mm_tn(yd[...], glow[...]))
    for k in range(2):
        rows = slice(k * count * enc, (k + 1) * count * enc)
        season_grad = mm_nt(dks[rows, :], wck[...]).astype(bf).astype(f32)
        stream_grad = season_grad - season_of(season_grad, aet[...], enc, count)
        low = stream_grad.astype(bf)
        mem_grad[rows, :] = low
        season_grad = stream_grad + ffn_backward(low, w1, w2, slope, pre_grad, rows)
        stream_grad = season_grad - season_of(season_grad, aet[...], enc, count)
        dz1e[rows, :] = stream_grad
        low = stream_grad.astype(bf)
        glow_e[rows, :] = low
        series = mm_nt(low, woe[...]).astype(bf)
        for i in range(count):
            start = (k * count + i) * 2 * modes
            value = mm(gte[...], series[i * enc : (i + 1) * enc])
            set_rows(scratch, slice(start, start + 2 * modes), value)
    to_partner(s, scratch, gy_own, gy_give, span, items, modes)
    sender.whole(0, 128, mm_tn(ye[...], glow_e[...]))
    low_t[...] = s1e[...].T
    grad_t[...] = mem_grad[...].T
    sender.ffn(256, low_t, grad_t, pre_grad, hidden)
    sender.send(keep, give, sems)


def inputs_kernel(
    sc, dx_own, dx_back, xe, xd, dz1e, dz1d, we, wd, fe, fd,
    enc_keep, enc_give, dec_keep, dec_give, keep, give,
    scratch, dqs_e, dqs_d, line, buffer, sems,
):
    items, modes = dx_own.shape[1] // 2, dx_own.shape[0]
    span = items * 2 * modes
    s = sc[0]
    modes_to_items(dx_own, scratch, s * span, items, modes)
    modes_to_items(dx_back, scratch, (1 - s) * span, items, modes)
    sender = Sender(sc, buffer, buffer.shape[2] // 2)
    for layer, (x, dz, w, f, dqs, near_out, far_out) in enumerate(
        ((xe, dz1e, we, fe, dqs_e, enc_keep, enc_give), (xd, dz1d, wd, fd, dqs_d, dec_keep, dec_give))
    ):
        length = f.shape[0]
        half = length // 2
        for i in range(items):
            at = layer * span + i * 2 * modes
            rows = slice(i * length, (i + 1) * length)
            coeffs = get_rows(scratch, slice(at, at + 2 * modes)).astype(bf)
            dqs[rows, :] = mm(f[...], coeffs).astype(bf)
        total = dz[...] + mm_nt(dqs[...], w[...])
        for i in range(items):
            line[0:length, :] = total[i * length : (i + 1) * length]
            near_out[i] = line[pl.ds(pl.multiple_of(s * half, 8), half), :]
            far_out[i] = line[pl.ds(pl.multiple_of((1 - s) * half, 8), half), :].astype(bf)
        sender.whole(layer, 0, mm_tn(x[...], dqs[...]))
    sender.send(keep, give, sems)


def call(name, body, ins, outs, scratch=(), far_outs=0, flops=0):
    vmem = pl.BlockSpec(memory_space=pltpu.VMEM)
    out_specs = [vmem] * (len(outs) - far_outs) + [pl.BlockSpec(memory_space=pl.ANY)] * far_outs
    moved = sum(math.prod(a.shape) * a.dtype.itemsize for a in list(ins) + list(outs))
    return pl.pallas_call(
        body,
        out_shape=list(outs),
        in_specs=[pl.BlockSpec(memory_space=pltpu.SMEM)] + [vmem] * (len(ins) - 1),
        out_specs=out_specs,
        scratch_shapes=list(scratch),
        compiler_params=pltpu.CompilerParams(vmem_limit_bytes=VMEM),
        cost_estimate=pl.CostEstimate(flops=int(flops), bytes_accessed=moved, transcendentals=0),
        name=name,
    )(*ins)


def shaped(dtype, *shape):
    return jax.ShapeDtypeStruct(shape, dtype)


def mix_call(w, x_own, x_far):
    heads, total, lanes = w.shape
    modes, rows, width = x_own.shape
    count = modes // PIECES
    x_spec = pl.BlockSpec((count, rows, width), lambda i: (i, 0, 0))
    return pl.pallas_call(
        mix_kernel,
        grid=(PIECES,),
        out_shape=[shaped(bf, *x_own.shape)] * 2,
        in_specs=[pl.BlockSpec((heads, total // PIECES, lanes), lambda i: (0, i, 0)), x_spec, x_spec],
        out_specs=[x_spec, x_spec],
        compiler_params=pltpu.CompilerParams(vmem_limit_bytes=VMEM),
        cost_estimate=pl.CostEstimate(
            flops=4 * w.size * rows, bytes_accessed=2 * w.size + 8 * x_own.size, transcendentals=0
        ),
        name="mix",
    )(w, x_own, x_far)


def mix_back_call(places, w, x_own, x_far, g_own, g_far):
    heads, total, lanes = w.shape
    modes, rows, width = x_own.shape
    count = modes // PIECES
    x_spec = pl.BlockSpec((count, rows, width), lambda i, at: (i, 0, 0))
    part = total // PIECES
    dw = shaped(bf, PIECES, heads // 2, part, lanes)
    return pl.pallas_call(
        mix_back_kernel,
        grid_spec=pltpu.PrefetchScalarGridSpec(
            num_scalar_prefetch=1,
            grid=(PIECES,),
            in_specs=[pl.BlockSpec((heads, part, lanes), lambda i, at: (0, i, 0))] + [x_spec] * 4,
            out_specs=[
                x_spec,
                x_spec,
                pl.BlockSpec((1, heads // 2, part, lanes), lambda i, at: (at[1 + i], 0, 0, 0)),
                pl.BlockSpec((1, heads // 2, part, lanes), lambda i, at: (at[1 + PIECES + i], 0, 0, 0)),
            ],
        ),
        out_shape=[shaped(bf, *x_own.shape)] * 2 + [dw, dw],
        compiler_params=pltpu.CompilerParams(vmem_limit_bytes=VMEM),
        cost_estimate=pl.CostEstimate(
            flops=12 * w.size * rows, bytes_accessed=4 * w.size + 12 * x_own.size, transcendentals=0
        ),
        name="mix_back",
    )(places, w, x_own, x_far, g_own, g_far)


def swap(value):
    return lax.ppermute(value, "section", [(0, 1), (1, 0)])


def shift(value, axis, steps):
    stride, size, count = axis
    pairs = []
    for source in range(count):
        at = source // stride % size
        pairs.append((source, source + ((at + steps) % size - at) * stride))
    return lax.ppermute(value, "dp", pairs)


def add_up(parts, dtype):
    total = parts[0].astype(f32)
    for part in parts[1:]:
        total = total + part.astype(f32)
    return total.astype(dtype)


def reduce_pair(first, second, axes):
    x, y, z = axes
    pair = []
    for value, order in ((first, (x, y)), (second, (y, x))):
        value = value.reshape((order[0][1], order[1][1], z[1]) + value.shape[1:])
        for axis in order:
            got = [shift(value[k], axis, k) for k in range(1, axis[1])]
            value = add_up([value[0]] + got, bf)
        pair.append(value)
    pieces = [jnp.stack([value[k] for value in pair]) for k in range(z[1])]
    got = [shift(pieces[k], z, k) for k in range(1, z[1])]
    total = add_up([pieces[0]] + got, f32)
    return total[0][None], total[1][None]


def per_device(
    enc_input, dec_input, pred_grad, dataset_id, chan_mask, enc_modes, dec_modes,
    proj_query, mix_self, proj_output, ffn_inner, ffn_outer,
    cross_query, cross_key, cross_output, mix_cross, trend_weight, season_weight,
):
    section = lax.axis_index("section")
    first_section = section == 0
    dp = lax.axis_size("dp")
    me = lax.axis_index("dp")
    both, enc_len, width = enc_input.shape
    dec_len = dec_input.shape[1]
    variates = pred_grad.shape[2]
    items = both // 2
    modes = enc_modes.shape[0]
    hidden = ffn_inner.shape[2]

    fast = dp == PIECES
    axes = ((1, 2, dp), (2, 2, dp), (4, 4, dp))
    dest = jnp.arange(PIECES, dtype=jnp.int32)
    if fast:
        rx, ry, rz = ((dest // a[0] - me // a[0]) % a[1] for a in axes)
        places_x, places_y = rx * 8 + ry * 4 + rz, ry * 8 + rx * 4 + rz
    else:
        places_x = places_y = dest
    sc = jnp.concatenate([section[None].astype(jnp.int32), places_x, places_y]).astype(jnp.int32)

    def mine(value):
        return lax.dynamic_slice_in_dim(value, section * items, items, axis=0)

    def pair(value):
        other = swap(value)
        return jnp.where(first_section, value, other), jnp.where(first_section, other, value)

    def joined(value, axis):
        return jnp.concatenate(pair(value), axis=axis)

    wqe, wqd = pair(proj_query[0])
    woe, wod = pair(proj_output[0])
    w1e, w1d = pair(ffn_inner[0])
    w2e, w2d = pair(ffn_outer[0])
    wcq = joined(cross_query, 0)
    wck = joined(cross_key, 0)
    wco = joined(cross_output, 0)
    pad = ((0, 0), (0, 0), (0, WIDE - variates))
    tw = joined(jnp.pad(trend_weight, pad).transpose(1, 0, 2).reshape(-1, 3 * WIDE), 0)
    sw = joined(jnp.pad(season_weight, pad[1:]), 0)

    fe, fte, ge, gte = transform_tables(enc_modes, enc_len)
    fd, ftd, gd, gtd = transform_tables(dec_modes, dec_len)
    ae, aet = average_counts(enc_len)
    ad, adt = average_counts(dec_len)
    widths = 7 * (dataset_id == 0) + 321 * (dataset_id == 1) + 21 * (dataset_id == 2)
    columns = jnp.arange(variates, dtype=jnp.int32)
    mask = mine(((columns[None, :] < widths[:, None]) & (chan_mask == 1)).astype(f32))
    xe = mine(enc_input).reshape(items * enc_len, width)
    xd = mine(dec_input).reshape(items * dec_len, width)
    cotangent = mine(pred_grad)

    ne, nd = items * enc_len, items * dec_len
    span = items * 2 * modes
    spectra = shaped(bf, modes, 2 * items, width)
    part_spectra = shaped(bf, modes, 2 * items, width // 2)
    mac = 2 * width

    x_own, x_give = call(
        "spectrum", spectrum_kernel, (sc, xe, xd, wqe, wqd, fte, ftd), (spectra, spectra),
        [pltpu.VMEM((width // 128, 2 * span, 128), f32)], flops=mac * (ne + nd) * (width + 2 * modes),
    )
    x_far = swap(x_give)
    y_own, y_far = mix_call(mix_self[0], x_own, x_far)
    y_back = swap(y_far)

    (ye, yd, s1e, hid_e, slope_e, memory, kc, s1d, t1d, qc, act, act_slope, v_own, v_give) = call(
        "middle", middle_kernel,
        (sc, y_own, y_back, xe, xd, woe, wod, w1e, w2e, wck, wcq, ge, gd, fte, ftd, ae, ad),
        (
            shaped(bf, ne, width), shaped(bf, nd, width), shaped(bf, ne, width),
            shaped(bf, ne, hidden), shaped(bf, ne, hidden), shaped(bf, ne, width),
            shaped(bf, items, 2 * modes, width), shaped(f32, nd, width), shaped(f32, nd, width),
            shaped(bf, items, 2 * modes, width), shaped(bf, items, HEADS, modes, 128),
            shaped(bf, items, HEADS, modes, 128), part_spectra, part_spectra,
        ),
        [pltpu.VMEM((width // 128, 2 * span, 128), f32), pltpu.VMEM((width // 256, 2 * span, 128), f32)],
        flops=mac * (ne * (2 * hidden + 2 * width + 4 * modes) + nd * (2 * width + 4 * modes)),
    )
    v_far = swap(v_give)
    yc_own, yc_far = mix_call(mix_cross, v_own, v_far)
    yc_back = swap(yc_far)

    group = shaped(bf, PIECES, ROWS, 128)
    half = dec_len // 2
    out_keep, out_give = shaped(f32, items, half, variates), shaped(bf, items, half, variates)
    low_rows = pltpu.VMEM((nd, width), bf)
    pred_keep, pred_give, trend_keep, trend_give, dz2, du, gc_own, gc_give, keep1, give1 = call(
        "outputs", outputs_kernel,
        (sc, yc_own, yc_back, s1d, t1d, wco, w1d, w2d, tw, sw, mask, cotangent, gd, gtd, ad, adt),
        (
            out_keep, out_give, out_keep, out_give, shaped(f32, nd, width), shaped(f32, nd, width),
            part_spectra, part_spectra, group, group,
        ),
        [
            pltpu.VMEM((width // 256, 2 * span, 128), f32), low_rows, low_rows, pltpu.VMEM((8, 128), f32),
            low_rows, pltpu.VMEM((nd, hidden), bf), pltpu.VMEM((nd, hidden), bf),
            pltpu.VMEM((nd, 3 * WIDE), bf), low_rows, low_rows, low_rows, low_rows,
            pltpu.VMEM((width, nd), bf), pltpu.VMEM((width, nd), bf),
            pltpu.VMEM((dec_len, WIDE), f32), pltpu.VMEM((dec_len, WIDE), f32),
            pltpu.VMEM((2, PIECES, ROWS, 128), bf), pltpu.SemaphoreType.DMA((2,)),
        ],
        far_outs=2, flops=mac * nd * (6 * hidden + 3 * width + 12 * WIDE + 4 * modes),
    )
    gc_far = swap(gc_give)
    dv_own, dv_far, cross_a, cross_b = mix_back_call(sc, mix_cross, v_own, v_far, gc_own, gc_far)
    dv_back = swap(dv_far)

    dz1d, dz1e, gy_own, gy_give, keep3, give3 = call(
        "cross_back", cross_back_kernel,
        (
            sc, dv_own, dv_back, qc, kc, act, act_slope, s1d, dz2, du, memory, wcq, wck, fd, fe,
            adt, aet, yd, ye, wod, woe, gtd, gte, hid_e, slope_e, s1e, w1e, w2e,
        ),
        (shaped(f32, nd, width), shaped(f32, ne, width), spectra, spectra, group, group),
        [
            pltpu.VMEM((width // 256, 2 * span, 128), f32), pltpu.VMEM((width // 128, 2 * span, 128), f32),
            pltpu.VMEM((items, 2 * modes, width), bf), pltpu.VMEM((items, 2 * modes, width), bf),
            low_rows, pltpu.VMEM((ne, width), bf), low_rows, pltpu.VMEM((ne, hidden), bf),
            pltpu.VMEM((width, ne), bf), pltpu.VMEM((width, ne), bf), pltpu.VMEM((ne, width), bf),
            pltpu.VMEM((ne, width), bf),
            pltpu.VMEM((2, PIECES, ROWS, 128), bf), pltpu.SemaphoreType.DMA((2,)),
        ],
        far_outs=2, flops=mac * (ne * (4 * hidden + 5 * width) + nd * 5 * width),
    )
    gy_far = swap(gy_give)
    dx_own, dx_far, self_a, self_b = mix_back_call(sc, mix_self[0], x_own, x_far, gy_own, gy_far)
    dx_back = swap(dx_far)

    small = shaped(bf, PIECES, 128, 128)
    enc_half = enc_len // 2
    enc_keep, enc_give, dec_keep, dec_give, keep5, give5 = call(
        "inputs", inputs_kernel, (sc, dx_own, dx_back, xe, xd, dz1e, dz1d, wqe, wqd, fe, fd),
        (
            shaped(f32, items, enc_half, width), shaped(bf, items, enc_half, width),
            shaped(f32, items, half, width), shaped(bf, items, half, width), small, small,
        ),
        [
            pltpu.VMEM((width // 128, 2 * span, 128), f32), pltpu.VMEM((ne, width), bf), low_rows,
            pltpu.VMEM((dec_len, width), f32), pltpu.VMEM((2, PIECES, 128, 128), bf),
            pltpu.SemaphoreType.DMA((2,)),
        ],
        far_outs=2, flops=mac * (ne + nd) * (2 * width + 2 * modes),
    )

    def group_sum(keep, give, cut):
        total = add_up([keep, swap(give)], bf)
        if not fast:
            return total
        return jnp.concatenate(reduce_pair(total[:, :cut], total[:, cut:], axes), axis=1)

    def mix_sum(first, second):
        if fast:
            first, second = reduce_pair(first, second, axes)
        value = jnp.concatenate([first, second], axis=1)
        value = value.transpose(1, 0, 2, 3).reshape(value.shape[1], -1, value.shape[3])
        return value if fast else lax.psum_scatter(value.astype(f32), "dp", scatter_dimension=1, tiled=True)

    def rows_of(group_value, row, lanes, part):
        count = lanes // 128
        value = group_value[:, row : row + count * part]
        value = value.reshape(-1, count, part, 128).transpose(0, 2, 1, 3)
        return value.reshape(-1, lanes)

    def scattered(value, axis=0):
        if fast:
            return value.astype(f32)
        return lax.psum_scatter(value.astype(f32), "dp", scatter_dimension=axis, tiled=True)

    group1 = group_sum(keep1, give1, CUT)
    grad_mix_cross = mix_sum(cross_a, cross_b)
    group3 = group_sum(keep3, give3, CUT)
    grad_mix_self = mix_sum(self_a, self_b)
    group5 = group_sum(keep5, give5, 64)

    thin = width // (2 * PIECES)
    part = width // PIECES
    grad_cross_output = scattered(rows_of(group1, 0, width, thin))
    trend_grad = rows_of(group1, 64, 3 * WIDE, thin).reshape(-1, 3, WIDE)[:, :, :variates]
    grad_trend = scattered(trend_grad.transpose(1, 0, 2), 1)
    grad_season = scattered(rows_of(group1, 208, WIDE, thin)[:, :variates])
    grad_cross_query = scattered(rows_of(group3, 0, width, thin))
    grad_cross_key = scattered(rows_of(group3, 64, width, thin))
    grad_proj_output = scattered(rows_of(group3, 128, width, part))
    grad_proj_query = scattered(rows_of(group5, 0, width, part))

    dec_ffn, enc_ffn = group1[:, 256:], group3[:, 256:]
    got = swap(jnp.where(first_section, dec_ffn, enc_ffn))
    inner = jnp.where(first_section, enc_ffn, got)
    outer = jnp.where(first_section, got, dec_ffn)
    grad_inner = scattered(rows_of(inner, 0, hidden, part))
    grad_outer = scattered(outer.transpose(0, 2, 1).reshape(-1, width))

    def output(keep, give):
        got = swap(give).astype(f32)
        return jnp.where(
            first_section, jnp.concatenate([keep, got], axis=0), jnp.concatenate([got, keep], axis=0)
        )

    return (
        output(pred_keep, pred_give),
        output(trend_keep, trend_give),
        output(enc_keep, enc_give),
        output(dec_keep, dec_give),
        grad_proj_query[None],
        grad_mix_self[None],
        grad_proj_output[None],
        grad_inner[None],
        grad_outer[None],
        grad_cross_query,
        grad_cross_key,
        grad_cross_output,
        grad_mix_cross,
        grad_trend,
        grad_season,
    )


def solution(mesh):
    in_specs = (
        P("dp", None, None),
        P("dp", None, None),
        P("dp", None, None),
        P("dp"),
        P("dp", None),
        P(),
        P(),
        P("section", None, None),
        P("section", None, None, None),
        P("section", None, None),
        P("section", None, None),
        P("section", None, None),
        P("section", None),
        P("section", None),
        P("section", None),
        P("section", None, None),
        P(None, "section", None),
        P("section", None),
    )
    out_specs = (
        P("dp", "section", None),
        P("dp", "section", None),
        P("dp", "section", None),
        P("dp", "section", None),
        P("section", "dp", None),
        P("section", None, "dp", None),
        P("section", "dp", None),
        P("section", "dp", None),
        P("section", "dp", None),
        P(("section", "dp"), None),
        P(("section", "dp"), None),
        P(("section", "dp"), None),
        P("section", "dp", None),
        P(None, ("section", "dp"), None),
        P(("section", "dp"), None),
    )
    return jax.shard_map(
        per_device, mesh=mesh, in_specs=in_specs, out_specs=out_specs, check_vma=False
    )
```
